32 devices in a mesh: ctx: 8 (over z, x), head: 4 (over y, core).
Axes of the slice: x: 2, y: 2, z: 4, core: 2. Of those that a mesh axis runs over, the one named last changes fastest.
Arguments:
- asking_vectors: bfloat16 [4096, 2048], P('ctx', 'head'), may hold values from -6 to 6
- lookup_vectors: bfloat16 [4096, 2048], P('ctx', 'head'), may hold values from -16 to 16
- payload_vectors: bfloat16 [4096, 2048], P('ctx', 'head'), may hold values from -16 to 16
- segment_owner_ids: int32 [16], P('ctx'), may hold values from 0 to 3, never falling along the last dimension, each value on 1 to 12 neighbouring positions
- attender_logit_factor: float32 [16], P('head'), may hold values from 4 to 16
- tier_logit_shift: float32 [16], P('head'), may hold values from -0.2 to 0.4
- final_projection_weights: bfloat16 [2048, 4096], P('head'), may hold values from -0.125 to 0.125
Outputs:
- mixed: bfloat16 [4096, 4096], P('ctx', 'head')
The draws below stay inside these ranges and needn't reach their ends.
All inputs are finite; a program needn't handle non-finite values.
Results may differ from the reference program's by a relative error of at most 0.011.
Values may be sent and summed in bfloat16 or wider, within the bound.
A program may use at most 64 MiB of HBM per device.

```python
import math
import jax
import jax.numpy as jnp
import numpy as np
from jax import lax

D = 4096
SHARD_ATTENDERS = 16
ATTN_DIMENSION = 128
BLOCK = 256
HEADS_DEV = 4
TOKENS = 4096
NB = 16
FAR = 3
N_HEAD = 4


def layered(key, salt, columns, ratio):
    seeded = jax.random.fold_in(key, salt)
    scales = TOKENS.bit_length() - 1
    summed = jnp.zeros((TOKENS, columns), jnp.float32)
    stretch = 1
    power_sum = 0.0
    for layer in range(scales):
        layer_key = jax.random.fold_in(seeded, layer)
        factor = ratio ** layer
        power_sum = power_sum + factor * factor
        pieces = jax.random.truncated_normal(layer_key, -3.0, 3.0, (TOKENS // stretch, columns), jnp.float32)
        spread = jnp.broadcast_to(pieces[:, None, :], (TOKENS // stretch, stretch, columns))
        summed = summed + factor * spread.reshape(TOKENS, columns)
        stretch = stretch * 2
    return summed / math.sqrt(power_sum)


def shared_direction(key):
    return jax.random.rademacher(jax.random.fold_in(key, 501), (SHARD_ATTENDERS * ATTN_DIMENSION,), jnp.float32)


def shared_level(key):
    coefficient = layered(key, 37, SHARD_ATTENDERS, 0.9)
    return jnp.repeat(coefficient, ATTN_DIMENSION, axis=1)


def key_rest(key):
    rest = layered(key, 11, SHARD_ATTENDERS * ATTN_DIMENSION, 0.9)
    return rest


def draw_lookup_vectors(key, part):
    direction = shared_direction(key)
    summed = 1.2 * shared_level(key) * direction[None, :] + 0.8 * key_rest(key)
    return jnp.clip(summed, -15.0, 15.0).astype(jnp.bfloat16)


def draw_payload_vectors(key, part):
    direction = shared_direction(key)
    own = layered(key, 23, SHARD_ATTENDERS * ATTN_DIMENSION, 0.9)
    summed = 0.9 * shared_level(key) * direction[None, :] + 0.5 * key_rest(key) + 0.6 * own
    return jnp.clip(summed, -15.0, 15.0).astype(jnp.bfloat16)


def draw_asking_vectors(key, part):
    direction = shared_direction(key)
    columns = SHARD_ATTENDERS * ATTN_DIMENSION
    strength_key = jax.random.fold_in(key, 61)
    noise_key = jax.random.fold_in(key, 67)
    strength = jax.random.truncated_normal(strength_key, -2.5, 2.5, (TOKENS, SHARD_ATTENDERS), jnp.float32)
    noise = jax.random.truncated_normal(noise_key, -3.0, 3.0, (TOKENS, columns), jnp.float32)
    summed = 1.5 * jnp.repeat(strength, ATTN_DIMENSION, axis=1) * direction[None, :] + noise
    return jnp.clip(summed, -6.0, 6.0).astype(jnp.bfloat16)


def shard_levels(rng, shape, cuts, low, largest):
    def one(position, parts):
        heights = jax.random.uniform(jax.random.fold_in(jax.random.fold_in(rng, 6), position), (parts,), jnp.float32, low / len(cuts), largest / len(cuts))
        return jnp.repeat(jnp.exp(heights), shape[position] // parts).reshape((-1,) + (1,) * (len(shape) - position - 1))

    level = one(*cuts[0])
    for cut in cuts[1:]:
        level = level * one(*cut)
    return level


def length_profile(amount, total, bound, lean):
    loads = [(1 << 20) // math.isqrt(grade ** lean) + 1 for grade in range(2, amount + 1)]
    surplus, given = total - bound - (amount - 1), [1] * (amount - 1)
    while surplus > 0:
        candidates = [i for i in range(amount - 1) if given[i] < bound]
        pool, left = sum([loads[i] for i in candidates]), surplus
        for i in candidates:
            more = min(bound - given[i], max(1, left * loads[i] // pool), surplus)
            given[i] = given[i] + more
            surplus = surplus - more
    return np.array([bound] + given)


def ragged(stream_key, count, total, reach, skew):
    if count == 2:
        one = jax.random.randint(stream_key, (), max(1, total - reach), min(reach, total - 1) + 1)
        return jnp.stack([one, total - one])
    sizes = jnp.asarray(length_profile(count, total, reach, skew), jnp.int32)
    pairs = (count - 1) // 2
    giver, taker = sizes[1:1 + 2 * pairs:2], sizes[2:2 + 2 * pairs:2]
    room = jnp.minimum(giver - 1, reach - taker)
    moved = jax.random.randint(jax.random.fold_in(stream_key, 1), (pairs,), 0, 1 << 20) % (room + 1)
    sizes = sizes.at[1:1 + 2 * pairs:2].set(giver - moved).at[2:2 + 2 * pairs:2].set(taker + moved)
    return sizes[jax.random.permutation(jax.random.fold_in(stream_key, 2), count)]


def gaussian(key, shape, scale, bound, cuts=(), held_as=jnp.bfloat16):
    values = jax.random.normal(key, shape, jnp.float32) * scale
    if len(cuts) > 0:
        values = shard_levels(key, shape, cuts, -0.22, 0.18) * values
    return jnp.clip(values, min=-bound, max=bound).astype(held_as)


def setup_inputs(seed: int = 0) -> dict:
    arg_keys = jax.random.split(jax.random.key(seed), 8)
    return {
        "asking_vectors": draw_asking_vectors(jax.random.fold_in(arg_keys[7], 71), 0),
        "lookup_vectors": draw_lookup_vectors(jax.random.fold_in(arg_keys[7], 71), 0),
        "payload_vectors": draw_payload_vectors(jax.random.fold_in(arg_keys[7], 71), 0),
        "segment_owner_ids": jnp.searchsorted(jnp.cumsum(ragged(arg_keys[3], NB // 4, NB, 12, 1)), jnp.arange(NB), side="right").astype(jnp.int32),
        "attender_logit_factor": jnp.clip(jnp.exp(math.log(16.0) - 1.3862944 * jax.random.uniform(arg_keys[4], (SHARD_ATTENDERS,), jnp.float32) ** shard_levels(arg_keys[4], (SHARD_ATTENDERS,), ((0, 4),), -0.2, 0.2)), 4.0, 16.0),
        "tier_logit_shift": jnp.clip(-0.2 + 0.6 * jax.random.uniform(arg_keys[5], (SHARD_ATTENDERS,), jnp.float32) ** shard_levels(arg_keys[5], (SHARD_ATTENDERS,), ((0, 4),), -0.2, 0.2), -0.2, 0.4),
        "final_projection_weights": gaussian(arg_keys[6], (SHARD_ATTENDERS * ATTN_DIMENSION, D), (SHARD_ATTENDERS * ATTN_DIMENSION) ** -0.5, 0.125, ((0, 4),)),
    }


EPS = 1e-06

def unit_rows(matrix):
    return matrix * lax.rsqrt(lax.optimization_barrier(jnp.mean(matrix * matrix, axis=-1, keepdims=True)) + EPS)

def run_means(matrix, attender_dimension):
    shaped = matrix.reshape((matrix.shape[0] // attender_dimension, attender_dimension) + matrix.shape[1:])
    return lax.optimization_barrier(jnp.mean(shaped, axis=1))

def attend(query_rows, key_rows, value_rows, logit_multiplier, offset, keep, numer, denom):
    scores = jnp.einsum('qhd,khd->hqk', query_rows.astype(jnp.float32), key_rows.astype(jnp.float32))
    weights = jnp.exp(scores * logit_multiplier[:, None, None] + offset[:, None, None]) * keep
    denom = denom + jnp.transpose(lax.optimization_barrier(jnp.sum(weights, axis=-1)))
    rounded = lax.optimization_barrier(weights.astype(jnp.bfloat16)).astype(jnp.float32)
    numer = numer + jnp.einsum('hqk,khd->qhd', rounded, value_rows.astype(jnp.float32))
    return (numer, denom)

def reference(asking_vectors, lookup_vectors, payload_vectors, segment_owner_ids, attender_logit_factor, tier_logit_shift, final_projection_weights):
    q_unit = unit_rows(asking_vectors.astype(jnp.float32).reshape(TOKENS, SHARD_ATTENDERS, ATTN_DIMENSION)).astype(jnp.bfloat16)
    k_unit = unit_rows(lookup_vectors.astype(jnp.float32).reshape(TOKENS, SHARD_ATTENDERS, ATTN_DIMENSION))
    k_near = k_unit.astype(jnp.bfloat16)
    v_near = payload_vectors.reshape(TOKENS, SHARD_ATTENDERS, ATTN_DIMENSION)
    v_wide = v_near.astype(jnp.float32)
    logit_multiplier = attender_logit_factor / ATTN_DIMENSION
    coarse_keys = []
    coarse_values = []
    for level in range(1, FAR + 1):
        span = 2 ** level
        coarse_keys.append(run_means(k_unit, span).astype(jnp.bfloat16).reshape(NB // span, BLOCK, SHARD_ATTENDERS, ATTN_DIMENSION))
        coarse_values.append(run_means(v_wide, span).astype(jnp.bfloat16).reshape(NB // span, BLOCK, SHARD_ATTENDERS, ATTN_DIMENSION))

    def one_block(index):
        start = index * BLOCK
        partner = jnp.bitwise_xor(index, 1)
        other = partner * BLOCK
        query_rows = lax.dynamic_slice_in_dim(q_unit, start, BLOCK, 0)
        numer = jnp.zeros((BLOCK, SHARD_ATTENDERS, ATTN_DIMENSION), jnp.float32)
        denom = jnp.zeros((BLOCK, SHARD_ATTENDERS), jnp.float32)
        still = jnp.zeros((SHARD_ATTENDERS,), jnp.float32)
        numer, denom = attend(query_rows, lax.dynamic_slice_in_dim(k_near, start, BLOCK, 0), lax.dynamic_slice_in_dim(v_near, start, BLOCK, 0), logit_multiplier, still, 1.0, numer, denom)
        keep = (segment_owner_ids[index] == segment_owner_ids[partner]).astype(jnp.float32)
        numer, denom = attend(query_rows, lax.dynamic_slice_in_dim(k_near, other, BLOCK, 0), lax.dynamic_slice_in_dim(v_near, other, BLOCK, 0), logit_multiplier, still, keep, numer, denom)
        for level in range(1, FAR + 1):
            node = jnp.bitwise_xor(jnp.right_shift(index, level), 1)
            numer, denom = attend(query_rows, coarse_keys[level - 1][node], coarse_values[level - 1][node], logit_multiplier, -level * tier_logit_shift, 1.0, numer, denom)
        return (numer / denom[:, :, None]).astype(jnp.bfloat16)
    attended = lax.map(one_block, jnp.arange(NB, dtype=jnp.int32)).reshape(TOKENS, SHARD_ATTENDERS * ATTN_DIMENSION)
    group = HEADS_DEV * ATTN_DIMENSION
    mixed = jnp.zeros((TOKENS, D), jnp.float32)
    for member in range(N_HEAD):
        part = jnp.dot(attended[:, member * group:(member + 1) * group], final_projection_weights[member * group:(member + 1) * group], preferred_element_type=jnp.float32)
        mixed = mixed + lax.optimization_barrier(part.astype(jnp.bfloat16)).astype(jnp.float32)
    return mixed.astype(jnp.bfloat16)
```

```python
import functools
import math

import jax
import jax.numpy as jnp
from jax import lax
from jax.experimental import pallas as pl
from jax.experimental.pallas import tpu as pltpu
from jax.sharding import PartitionSpec as P

EPS = 1e-06
BF16 = jnp.bfloat16
F32 = jnp.float32
TILE = 128
MESH = pl.DeviceIdType.MESH


def dot(a, b):
    return jnp.dot(a, b, preferred_element_type=F32)


def dot_t(a, b):
    return lax.dot_general(a, b, (((1,), (1,)), ((), ())), preferred_element_type=F32)


def unit(rows):
    return rows * lax.rsqrt(jnp.mean(rows * rows, axis=-1, keepdims=True) + EPS)


def kernel(
    n_ctx, n_head, heads, blocks,
    q_hbm, k_hbm, v_hbm, seg, factor, shift, w_hbm,
    out_ref,
    q_raw, k_raw, v_raw, q_s, k_hi, k_lo, acc, att, w_v, y_send, y_recv, own,
    load_sem, kv_send_sem, kv_recv_sem, w_send_sem, w_recv_sem,
    att_send_sem, att_recv_sem, y_send_sem, y_recv_sem, *pieces,
):
    rows, width = q_raw.shape
    dim = width // heads
    block_rows = rows // blocks
    out_cols = out_ref.shape[1]
    steps = n_ctx.bit_length() - 1
    local_levels = blocks.bit_length() - 1
    send, recv = pieces[:steps], pieces[steps:]
    chunks = rows // TILE

    place = lax.axis_index("ctx")
    h = lax.axis_index("head")
    h1 = h + 1 - 2 * (h % 2)
    h2 = (h + 2) % n_head
    h3 = (h1 + 2) % n_head

    k_load = pltpu.make_async_copy(k_hbm, k_raw, load_sem.at[0])
    v_load = pltpu.make_async_copy(v_hbm, v_raw, load_sem.at[1])
    q_load = pltpu.make_async_copy(q_hbm, q_raw, load_sem.at[2])
    k_load.start()
    v_load.start()
    q_load.start()

    barrier = pltpu.get_barrier_semaphore()
    for i in range(1, n_ctx):
        pl.semaphore_signal(
            barrier, inc=1, device_id={"ctx": (place + i) % n_ctx}, device_id_type=MESH
        )
    for peer in (h1, h2):
        pl.semaphore_signal(barrier, inc=1, device_id={"head": peer}, device_id_type=MESH)

    def cols(index):
        return pl.ds(pl.multiple_of(index * out_cols, out_cols), out_cols)

    w_loads = []
    for i, block in enumerate((h, h2)):
        load = pltpu.make_async_copy(
            w_hbm.at[:, cols(block)], w_v.at[i, pl.ds(0, width)], load_sem.at[3 + i]
        )
        load.start()
        w_loads.append(load)

    k_load.wait()

    @pl.loop(0, rows // 64)
    def _(r):
        at = pl.ds(pl.multiple_of(r * 64, 64), 64)
        for a in range(heads):
            c = slice(a * dim, (a + 1) * dim)
            normed = unit(k_raw[at, c].astype(F32))
            high = normed.astype(BF16)
            k_hi[at, c] = high
            k_lo[at, c] = (normed - high.astype(F32)).astype(BF16)

    v_load.wait()
    pl.semaphore_wait(barrier, n_ctx + 1)

    kv_copies = []
    for s in reversed(range(steps)):
        span = 2 ** (local_levels + s)
        count = rows // span
        members = 2**s
        gap = lax.broadcasted_iota(jnp.int32, (count, rows), 1) - span * lax.broadcasted_iota(
            jnp.int32, (count, rows), 0
        )
        average = jnp.where((gap >= 0) & (gap < span), 1.0 / span, 0.0).astype(BF16)
        mean_k = dot(average, k_hi[...]) + dot(average, k_lo[...])
        send[s][:, :width] = mean_k.astype(BF16).astype(send[s].dtype)
        send[s][:, width:] = dot(average, v_raw[...]).astype(BF16).astype(send[s].dtype)
        group = place // members
        sibling = group + 1 - 2 * (group % 2)
        mine = place % members
        for j in range(members):
            copy = pltpu.make_async_remote_copy(
                src_ref=send[s],
                dst_ref=recv[s].at[pl.ds(pl.multiple_of(mine * count, count), count)],
                send_sem=kv_send_sem.at[members - 1 + j],
                recv_sem=kv_recv_sem.at[members - 1 + mine],
                device_id={"ctx": sibling * members + (mine + j) % members},
                device_id_type=MESH,
            )
            copy.start()
            kv_copies.append(copy)

    w_copies = []
    for i, block in enumerate((h1, h3)):
        copy = pltpu.make_async_remote_copy(
            src_ref=w_hbm.at[:, cols(block)],
            dst_ref=w_v.at[i, pl.ds(width, width)],
            send_sem=w_send_sem.at[i],
            recv_sem=w_recv_sem.at[i],
            device_id={"head": h1},
            device_id_type=MESH,
        )
        copy.start()
        w_copies.append(copy)

    q_load.wait()

    @pl.loop(0, rows // 64)
    def _(r):
        at = pl.ds(pl.multiple_of(r * 64, 64), 64)
        for a in range(heads):
            c = slice(a * dim, (a + 1) * dim)
            scale = factor[a] * (math.log2(math.e) / dim)
            q_s[at, c] = (unit(q_raw[at, c].astype(F32)) * scale).astype(BF16)

    ones = jnp.ones((block_rows, dim), BF16)

    def tile(query, keys, values):
        probs = jnp.exp2(dot_t(query, keys)).astype(BF16)
        return dot(probs, jnp.concatenate([values, ones], axis=1))

    for b in range(blocks):
        o = b ^ 1
        keep = jnp.where(seg[b] == seg[o], 1.0, 0.0).astype(F32)
        here = slice(b * block_rows, (b + 1) * block_rows)
        there = slice(o * block_rows, (o + 1) * block_rows)

        @pl.loop(0, block_rows // TILE)
        def _(r):
            at = pl.ds(pl.multiple_of(b * block_rows + r * TILE, TILE), TILE)
            for a in range(heads):
                c = slice(a * dim, (a + 1) * dim)
                query = q_s[at, c]
                acc[a, at, :] = tile(query, k_hi[here, c], v_raw[here, c]) + keep * tile(
                    query, k_hi[there, c], v_raw[there, c]
                )

    def wait_step(s):
        members = 2**s
        count = block_rows // members
        for j in range(members):
            pltpu.make_async_remote_copy(
                src_ref=send[s],
                dst_ref=recv[s].at[pl.ds(j * count, count)],
                send_sem=kv_send_sem.at[members - 1 + j],
                recv_sem=kv_recv_sem.at[members - 1 + j],
                device_id={"ctx": place},
                device_id_type=MESH,
            ).wait_recv()

    def far(s, a, at):
        level = local_levels + s
        c = slice(a * dim, (a + 1) * dim)
        cv = slice(width + a * dim, width + (a + 1) * dim)
        decay = jnp.exp(jnp.full((1, 2 * dim), -level * shift[a], F32))
        keys, values = recv[s][:, c].astype(BF16), recv[s][:, cv].astype(BF16)
        return acc[a, at, :] + decay * tile(q_s[at, c], keys, values)

    for s in reversed(range(1, steps)):
        wait_step(s)

        @pl.loop(0, chunks)
        def _(r):
            at = pl.ds(pl.multiple_of(r * TILE, TILE), TILE)
            for a in range(heads):
                acc[a, at, :] = far(s, a, at)

    wait_step(0)

    def project(r, i):
        at = slice(r * TILE, (r + 1) * TILE)
        return dot(att[0, at, :], w_v[i, :width, :]) + dot(att[1, at, :], w_v[i, width:, :])

    att_copies, y_copies = [], []
    for r in range(chunks + 1):
        if r < chunks:
            at = slice(r * TILE, (r + 1) * TILE)
            for a in range(heads):
                total = far(0, a, at)
                att[0, at, a * dim : (a + 1) * dim] = (total[:, :dim] / total[:, dim:]).astype(BF16)
            copy = pltpu.make_async_remote_copy(
                src_ref=att.at[0, pl.ds(r * TILE, TILE)],
                dst_ref=att.at[1, pl.ds(r * TILE, TILE)],
                send_sem=att_send_sem.at[r],
                recv_sem=att_recv_sem.at[r],
                device_id={"head": h1},
                device_id_type=MESH,
            )
            copy.start()
            att_copies.append(copy)
        if r >= 1:
            if r == 1:
                for i in (1, 0):
                    w_loads[i].wait()
                    w_copies[i].wait_recv()
            att_copies[r - 1].wait_recv()
            at = slice((r - 1) * TILE, r * TILE)
            y_send[at, :] = project(r - 1, 1).astype(BF16)
            copy = pltpu.make_async_remote_copy(
                src_ref=y_send.at[pl.ds((r - 1) * TILE, TILE)],
                dst_ref=y_recv.at[pl.ds((r - 1) * TILE, TILE)],
                send_sem=y_send_sem.at[r - 1],
                recv_sem=y_recv_sem.at[r - 1],
                device_id={"head": h2},
                device_id_type=MESH,
            )
            copy.start()
            y_copies.append(copy)

    for r in range(chunks):
        own[r * TILE : (r + 1) * TILE, :] = project(r, 0)
    for r in range(chunks):
        at = slice(r * TILE, (r + 1) * TILE)
        y_copies[r].wait_recv()
        out_ref[at, :] = (own[at, :] + y_recv[at, :].astype(F32)).astype(BF16)

    for copy in kv_copies + w_copies + att_copies + y_copies:
        copy.wait_send()


def per_device(n_ctx, n_head, q, k, v, seg, factor, shift, weights):
    rows, width = q.shape
    heads = factor.shape[0]
    blocks = seg.shape[0]
    block_rows = rows // blocks
    out_cols = weights.shape[1] // n_head
    steps = n_ctx.bit_length() - 1
    chunks = rows // TILE
    dim = width // heads

    def kind(s):
        return BF16 if (block_rows >> s) % 16 == 0 else F32

    hbm = pl.BlockSpec(memory_space=pltpu.HBM)
    smem = pl.BlockSpec(memory_space=pltpu.SMEM)
    dma = pltpu.SemaphoreType.DMA
    return pl.pallas_call(
        functools.partial(kernel, n_ctx, n_head, heads, blocks),
        out_shape=jax.ShapeDtypeStruct((rows, out_cols), BF16),
        in_specs=[hbm, hbm, hbm, smem, smem, smem, hbm],
        out_specs=pl.BlockSpec(memory_space=pltpu.VMEM),
        scratch_shapes=[
            *[pltpu.VMEM((rows, width), BF16)] * 6,
            pltpu.VMEM((heads, rows, 2 * dim), F32),
            pltpu.VMEM((2, rows, width), BF16),
            pltpu.VMEM((2, 2 * width, out_cols), BF16),
            pltpu.VMEM((rows, out_cols), BF16),
            pltpu.VMEM((rows, out_cols), BF16),
            pltpu.VMEM((rows, out_cols), F32),
            dma((5,)),
            dma((n_ctx - 1,)),
            dma((n_ctx - 1,)),
            dma((2,)),
            dma((2,)),
            dma((chunks,)),
            dma((chunks,)),
            dma((chunks,)),
            dma((chunks,)),
            *[pltpu.VMEM((block_rows >> s, 2 * width), kind(s)) for s in range(steps)],
            *[pltpu.VMEM((block_rows, 2 * width), kind(s)) for s in range(steps)],
        ],
        compiler_params=pltpu.CompilerParams(
            collective_id=0, has_side_effects=True, vmem_limit_bytes=48 * 1024 * 1024
        ),
        cost_estimate=pl.CostEstimate(
            flops=4 * 10**9, bytes_accessed=8 * 10**6, transcendentals=3 * 10**6
        ),
    )(q, k, v, seg, factor, shift, weights)


def solution(mesh):
    placed = (
        P("ctx", "head"),
        P("ctx", "head"),
        P("ctx", "head"),
        P("ctx"),
        P("head"),
        P("head"),
        P("head", None),
    )
    body = functools.partial(per_device, mesh.shape["ctx"], mesh.shape["head"])
    return jax.shard_map(
        body, mesh=mesh, in_specs=placed, out_specs=P("ctx", "head"), check_vma=False
    )
```

```python
import functools
import math

import jax
import jax.numpy as jnp
from jax import lax
from jax.experimental import pallas as pl
from jax.experimental.pallas import tpu as pltpu
from jax.sharding import PartitionSpec as P

EPS = 1e-06
BF16 = jnp.bfloat16
F32 = jnp.float32
TILE = 128
MESH = pl.DeviceIdType.MESH


def dot(a, b):
    return jnp.dot(a, b, preferred_element_type=F32)


def dot_t(a, b):
    return lax.dot_general(a, b, (((1,), (1,)), ((), ())), preferred_element_type=F32)


def flipped(index, bit):
    size = 2**bit
    return index + size - 2 * size * ((index // size) % 2)


def unit(rows):
    dim = rows.shape[1]
    squares = rows * rows
    high = squares.astype(BF16)
    low = (squares - high.astype(F32)).astype(BF16)
    total = dot(jnp.concatenate([high, low], axis=1), jnp.ones((2 * dim, dim), BF16))
    return rows * lax.rsqrt(total * (1.0 / dim) + EPS)


def row_chunks(rows):
    half = TILE // 2
    sizes = [half, half] + [TILE] * (rows // TILE - 2) + [half, half]
    return [(sum(sizes[:i]), size) for i, size in enumerate(sizes)]


def kernel(
    n_ctx, n_head, heads, blocks,
    q_hbm, k_hbm, v_hbm, seg, factor, shift, w_hbm,
    out_ref,
    q_raw, k_raw, v_raw, q_s, k_hi, average, acc, att, w_v, y_send, y_recv, own,
    load_sem, kv_send_sem, kv_recv_sem, w_send_sem, w_recv_sem,
    att_send_sem, att_recv_sem, y_send_sem, y_recv_sem, *pieces,
):
    rows, width = q_raw.shape
    dim = width // heads
    block_rows = rows // blocks
    out_cols = out_ref.shape[1]
    steps = n_ctx.bit_length() - 1
    local_levels = blocks.bit_length() - 1
    send, recv = pieces[:steps], pieces[steps:]
    chunks = row_chunks(rows)

    place = lax.axis_index("ctx")
    h = lax.axis_index("head")
    h1 = h + 1 - 2 * (h % 2)
    h2 = (h + 2) % n_head
    h3 = (h1 + 2) % n_head

    k_load = pltpu.make_async_copy(k_hbm, k_raw, load_sem.at[0])
    v_load = pltpu.make_async_copy(v_hbm, v_raw, load_sem.at[1])
    q_load = pltpu.make_async_copy(q_hbm, q_raw, load_sem.at[2])
    k_load.start()
    v_load.start()
    q_load.start()

    barrier = pltpu.get_barrier_semaphore()
    for bit in range(steps):
        pl.semaphore_signal(
            barrier, inc=1, device_id={"ctx": flipped(place, bit)}, device_id_type=MESH
        )
    for peer in (h1, h2):
        pl.semaphore_signal(barrier, inc=1, device_id={"head": peer}, device_id_type=MESH)

    def cols(index):
        return pl.ds(pl.multiple_of(index * out_cols, out_cols), out_cols)

    w_loads = []
    for i, block in enumerate((h, h2)):
        load = pltpu.make_async_copy(
            w_hbm.at[:, cols(block)], w_v.at[i, pl.ds(0, width)], load_sem.at[3 + i]
        )
        load.start()
        w_loads.append(load)

    tops = [sum(rows >> (local_levels + i) for i in range(s)) for s in range(steps)]
    for s in range(steps):
        span = 2 ** (local_levels + s)
        count = rows // span
        token = lax.broadcasted_iota(jnp.int32, (count, rows), 1)
        first = span * lax.broadcasted_iota(jnp.int32, (count, rows), 0)
        gap = token - first
        average[tops[s] : tops[s] + count, :] = jnp.where(
            (gap >= 0) & (gap < span), 1.0 / span, 0.0
        ).astype(BF16)

    k_load.wait()
    for r in range(0, rows, TILE):
        for a in range(heads):
            c = slice(a * dim, (a + 1) * dim)
            k_hi[r : r + TILE, c] = unit(k_raw[r : r + TILE, c].astype(F32)).astype(BF16)

    v_load.wait()
    pl.semaphore_wait(barrier, steps + 2)

    kv_copies = {}

    def hop(s, stage, src, first_row, count, bit):
        spot = s * (s + 1) // 2 + stage
        copy = pltpu.make_async_remote_copy(
            src_ref=src,
            dst_ref=recv[s].at[pl.ds(pl.multiple_of(first_row, count), count)],
            send_sem=kv_send_sem.at[spot],
            recv_sem=kv_recv_sem.at[spot],
            device_id={"ctx": flipped(place, bit)},
            device_id_type=MESH,
        )
        copy.start()
        kv_copies[s, stage] = copy

    def forward(s, stage):
        kv_copies[s, stage].wait_recv()
        size = 2**stage
        count = size * (block_rows >> s)
        first_row = (place % 2**s) // size * count
        held = recv[s].at[pl.ds(pl.multiple_of(first_row, count), count)]
        hop(s, stage + 1, held, first_row, count, stage)

    for s in reversed(range(steps)):
        count = block_rows >> s
        matrix = average[tops[s] : tops[s] + count, :]
        send[s][:, :width] = dot(matrix, k_hi[...]).astype(BF16).astype(send[s].dtype)
        send[s][:, width:] = dot(matrix, v_raw[...]).astype(BF16).astype(send[s].dtype)
        hop(s, 0, send[s], (place % 2**s) * count, count, s)

    w_copies = []
    for i, block in enumerate((h1, h3)):
        copy = pltpu.make_async_remote_copy(
            src_ref=w_hbm.at[:, cols(block)],
            dst_ref=w_v.at[i, pl.ds(width, width)],
            send_sem=w_send_sem.at[i],
            recv_sem=w_recv_sem.at[i],
            device_id={"head": h1},
            device_id_type=MESH,
        )
        copy.start()
        w_copies.append(copy)

    q_load.wait()

    for r in range(0, rows, TILE):
        for a in range(heads):
            c = slice(a * dim, (a + 1) * dim)
            scale = factor[a] * (math.log2(math.e) / dim)
            q_s[r : r + TILE, c] = (unit(q_raw[r : r + TILE, c].astype(F32)) * scale).astype(BF16)

    ones = jnp.ones((block_rows, dim), BF16)

    def tile(query, keys, values):
        probs = jnp.exp2(dot_t(query, keys)).astype(BF16)
        return dot(probs, jnp.concatenate([values, ones], axis=1))

    for b in range(blocks):
        o = b ^ 1
        keep = jnp.where(seg[b] == seg[o], 1.0, 0.0).astype(F32)
        here = slice(b * block_rows, (b + 1) * block_rows)
        there = slice(o * block_rows, (o + 1) * block_rows)

        @pl.loop(0, block_rows // TILE)
        def _(r):
            at = pl.ds(pl.multiple_of(b * block_rows + r * TILE, TILE), TILE)
            for a in range(heads):
                c = slice(a * dim, (a + 1) * dim)
                query = q_s[at, c]
                acc[a, at, :] = tile(query, k_hi[here, c], v_raw[here, c]) + keep * tile(
                    query, k_hi[there, c], v_raw[there, c]
                )

        if b == 0:
            for s in reversed(range(2, steps)):
                forward(s, 0)

    def far(s, a, at):
        level = local_levels + s
        c = slice(a * dim, (a + 1) * dim)
        cv = slice(width + a * dim, width + (a + 1) * dim)
        decay = jnp.exp(jnp.full((1, 2 * dim), -level * shift[a], F32))
        keys, values = recv[s][:, c].astype(BF16), recv[s][:, cv].astype(BF16)
        return acc[a, at, :] + decay * tile(q_s[at, c], keys, values)

    if steps > 1:
        forward(1, 0)
    for stage in range(1, steps):
        for s in reversed(range(stage + 1, steps)):
            forward(s, stage)
    last = min(1, steps - 1)
    for s in [s for s in [0, *reversed(range(2, steps))] if s != last]:
        kv_copies[s, s].wait_recv()

        @pl.loop(0, rows // TILE)
        def _(r):
            at = pl.ds(pl.multiple_of(r * TILE, TILE), TILE)
            for a in range(heads):
                acc[a, at, :] = far(s, a, at)

    kv_copies[last, last].wait_recv()

    def project(at, i):
        return dot(att[0, at, :], w_v[i, :width, :]) + dot(att[1, at, :], w_v[i, width:, :])

    att_copies, y_copies = [], []
    for r in range(len(chunks) + 1):
        if r < len(chunks):
            first, size = chunks[r]
            at = slice(first, first + size)
            for a in range(heads):
                total = far(last, a, at)
                att[0, at, a * dim : (a + 1) * dim] = (total[:, :dim] / total[:, dim:]).astype(BF16)
            copy = pltpu.make_async_remote_copy(
                src_ref=att.at[0, pl.ds(first, size)],
                dst_ref=att.at[1, pl.ds(first, size)],
                send_sem=att_send_sem.at[r],
                recv_sem=att_recv_sem.at[r],
                device_id={"head": h1},
                device_id_type=MESH,
            )
            copy.start()
            att_copies.append(copy)
        if r >= 1:
            if r == 1:
                for i in (1, 0):
                    w_loads[i].wait()
                    w_copies[i].wait_recv()
            att_copies[r - 1].wait_recv()
            first, size = chunks[r - 1]
            at = slice(first, first + size)
            y_send[at, :] = project(at, 1).astype(BF16)
            copy = pltpu.make_async_remote_copy(
                src_ref=y_send.at[pl.ds(first, size)],
                dst_ref=y_recv.at[pl.ds(first, size)],
                send_sem=y_send_sem.at[r - 1],
                recv_sem=y_recv_sem.at[r - 1],
                device_id={"head": h2},
                device_id_type=MESH,
            )
            copy.start()
            y_copies.append(copy)

    for first in range(0, rows, TILE):
        at = slice(first, first + TILE)
        own[at, :] = project(at, 0)
    for (first, size), copy in zip(chunks, y_copies):
        at = slice(first, first + size)
        copy.wait_recv()
        out_ref[at, :] = (own[at, :] + y_recv[at, :].astype(F32)).astype(BF16)

    for copy in list(kv_copies.values()) + w_copies + att_copies + y_copies:
        copy.wait_send()


def per_device(n_ctx, n_head, q, k, v, seg, factor, shift, weights):
    rows, width = q.shape
    heads = factor.shape[0]
    blocks = seg.shape[0]
    block_rows = rows // blocks
    out_cols = weights.shape[1] // n_head
    steps = n_ctx.bit_length() - 1
    chunks = len(row_chunks(rows))
    dim = width // heads
    hops = steps * (steps + 1) // 2

    def kind(s):
        return BF16 if (block_rows >> s) % 16 == 0 else F32

    hbm = pl.BlockSpec(memory_space=pltpu.HBM)
    smem = pl.BlockSpec(memory_space=pltpu.SMEM)
    dma = pltpu.SemaphoreType.DMA
    return pl.pallas_call(
        functools.partial(kernel, n_ctx, n_head, heads, blocks),
        out_shape=jax.ShapeDtypeStruct((rows, out_cols), BF16),
        in_specs=[hbm, hbm, hbm, smem, smem, smem, hbm],
        out_specs=pl.BlockSpec(memory_space=pltpu.VMEM),
        scratch_shapes=[
            *[pltpu.VMEM((rows, width), BF16)] * 5,
            pltpu.VMEM((rows, rows), BF16),
            pltpu.VMEM((heads, rows, 2 * dim), F32),
            pltpu.VMEM((2, rows, width), BF16),
            pltpu.VMEM((2, 2 * width, out_cols), BF16),
            pltpu.VMEM((rows, out_cols), BF16),
            pltpu.VMEM((rows, out_cols), BF16),
            pltpu.VMEM((rows, out_cols), F32),
            dma((5,)),
            dma((hops,)),
            dma((hops,)),
            dma((2,)),
            dma((2,)),
            dma((chunks,)),
            dma((chunks,)),
            dma((chunks,)),
            dma((chunks,)),
            *[pltpu.VMEM((block_rows >> s, 2 * width), kind(s)) for s in range(steps)],
            *[pltpu.VMEM((block_rows, 2 * width), kind(s)) for s in range(steps)],
        ],
        compiler_params=pltpu.CompilerParams(
            collective_id=0, has_side_effects=True, vmem_limit_bytes=64 * 1024 * 1024 - 65536
        ),
        cost_estimate=pl.CostEstimate(
            flops=4 * 10**9, bytes_accessed=8 * 10**6, transcendentals=3 * 10**6
        ),
    )(q, k, v, seg, factor, shift, weights)


def solution(mesh):
    placed = (
        P("ctx", "head"),
        P("ctx", "head"),
        P("ctx", "head"),
        P("ctx"),
        P("head"),
        P("head"),
        P("head", None),
    )
    body = functools.partial(per_device, mesh.shape["ctx"], mesh.shape["head"])
    return jax.shard_map(
        body, mesh=mesh, in_specs=placed, out_specs=P("ctx", "head"), check_vma=False
    )
```

```python
import functools
import math

import jax
import jax.numpy as jnp
from jax import lax
from jax.experimental import pallas as pl
from jax.experimental.pallas import tpu as pltpu
from jax.sharding import PartitionSpec as P

EPS = 1e-06
BF16 = jnp.bfloat16
F32 = jnp.float32
TILE = 128
MESH = pl.DeviceIdType.MESH


def dot(a, b):
    return jnp.dot(a, b, preferred_element_type=F32)


def dot_t(a, b):
    return lax.dot_general(a, b, (((1,), (1,)), ((), ())), preferred_element_type=F32)


def flipped(index, bit):
    size = 2**bit
    return index + size - 2 * size * ((index // size) % 2)


def unit(rows):
    dim = rows.shape[1]
    squares = rows * rows
    high = squares.astype(BF16)
    low = (squares - high.astype(F32)).astype(BF16)
    total = dot(jnp.concatenate([high, low], axis=1), jnp.ones((2 * dim, dim), BF16))
    return rows * lax.rsqrt(total * (1.0 / dim) + EPS)


def row_chunks(rows):
    half = TILE // 2
    sizes = [half, half] + [TILE] * (rows // TILE - 2) + [half, half]
    return [(sum(sizes[:i]), size) for i, size in enumerate(sizes)]


def kernel(
    n_ctx, n_head, heads, blocks,
    q_hbm, k_hbm, v_hbm, seg, factor, shift, w_hbm,
    out_ref,
    q_raw, k_raw, v_raw, q_s, k_hi, average, acc, att, w_v, y_send, y_recv, own,
    load_sem, kv_send_sem, kv_recv_sem, w_send_sem, w_recv_sem,
    att_send_sem, att_recv_sem, y_send_sem, y_recv_sem, *pieces,
):
    rows, width = q_raw.shape
    dim = width // heads
    block_rows = rows // blocks
    out_cols = out_ref.shape[1]
    steps = n_ctx.bit_length() - 1
    local_levels = blocks.bit_length() - 1
    send, recv = pieces[:steps], pieces[steps:]
    chunks = row_chunks(rows)

    place = lax.axis_index("ctx")
    h = lax.axis_index("head")
    h1 = h + 1 - 2 * (h % 2)
    h2 = (h + 2) % n_head
    h3 = (h1 + 2) % n_head

    k_load = pltpu.make_async_copy(k_hbm, k_raw, load_sem.at[0])
    v_load = pltpu.make_async_copy(v_hbm, v_raw, load_sem.at[1])
    q_load = pltpu.make_async_copy(q_hbm, q_raw, load_sem.at[2])
    k_load.start()
    v_load.start()
    q_load.start()

    barrier = pltpu.get_barrier_semaphore()
    for bit in range(steps):
        pl.semaphore_signal(
            barrier, inc=1, device_id={"ctx": flipped(place, bit)}, device_id_type=MESH
        )
    for peer in (h1, h2):
        pl.semaphore_signal(barrier, inc=1, device_id={"head": peer}, device_id_type=MESH)

    def cols(index):
        return pl.ds(pl.multiple_of(index * out_cols, out_cols), out_cols)

    w_loads = []
    for i, block in enumerate((h, h2)):
        load = pltpu.make_async_copy(
            w_hbm.at[:, cols(block)], w_v.at[i, pl.ds(0, width)], load_sem.at[3 + i]
        )
        load.start()
        w_loads.append(load)

    tops = [sum(rows >> (local_levels + i) for i in range(s)) for s in range(steps)]
    for s in range(steps):
        span = 2 ** (local_levels + s)
        count = rows // span
        token = lax.broadcasted_iota(jnp.int32, (count, rows), 1)
        first = span * lax.broadcasted_iota(jnp.int32, (count, rows), 0)
        gap = token - first
        average[tops[s] : tops[s] + count, :] = jnp.where(
            (gap >= 0) & (gap < span), 1.0 / span, 0.0
        ).astype(BF16)

    k_load.wait()
    for r in range(0, rows, TILE):
        for a in range(heads):
            c = slice(a * dim, (a + 1) * dim)
            k_hi[r : r + TILE, c] = unit(k_raw[r : r + TILE, c].astype(F32)).astype(BF16)

    v_load.wait()
    pl.semaphore_wait(barrier, steps + 2)

    kv_copies = {}

    def hop(s, stage, src, first_row, count, bit):
        spot = s * (s + 1) // 2 + stage
        copy = pltpu.make_async_remote_copy(
            src_ref=src,
            dst_ref=recv[s].at[pl.ds(pl.multiple_of(first_row, count), count)],
            send_sem=kv_send_sem.at[spot],
            recv_sem=kv_recv_sem.at[spot],
            device_id={"ctx": flipped(place, bit)},
            device_id_type=MESH,
        )
        copy.start()
        kv_copies[s, stage] = copy

    def forward(s, stage):
        kv_copies[s, stage].wait_recv()
        size = 2**stage
        count = size * (block_rows >> s)
        first_row = (place % 2**s) // size * count
        held = recv[s].at[pl.ds(pl.multiple_of(first_row, count), count)]
        hop(s, stage + 1, held, first_row, count, stage)

    for s in range(steps):
        count = block_rows >> s
        matrix = average[tops[s] : tops[s] + count, :]
        send[s][:, :width] = dot(matrix, k_hi[...]).astype(BF16).astype(send[s].dtype)
        send[s][:, width:] = dot(matrix, v_raw[...]).astype(BF16).astype(send[s].dtype)
        hop(s, 0, send[s], (place % 2**s) * count, count, s)

    w_copies = []
    for i, block in enumerate((h1, h3)):
        copy = pltpu.make_async_remote_copy(
            src_ref=w_hbm.at[:, cols(block)],
            dst_ref=w_v.at[i, pl.ds(width, width)],
            send_sem=w_send_sem.at[i],
            recv_sem=w_recv_sem.at[i],
            device_id={"head": h1},
            device_id_type=MESH,
        )
        copy.start()
        w_copies.append(copy)

    q_load.wait()

    for r in range(0, rows, TILE):
        for a in range(heads):
            c = slice(a * dim, (a + 1) * dim)
            scale = factor[a] * (math.log2(math.e) / dim)
            q_s[r : r + TILE, c] = (unit(q_raw[r : r + TILE, c].astype(F32)) * scale).astype(BF16)

    ones = jnp.ones((block_rows, dim), BF16)

    def tile(query, keys, values):
        probs = jnp.exp2(dot_t(query, keys)).astype(BF16)
        return dot(probs, jnp.concatenate([values, ones], axis=1))

    for b in range(blocks):
        o = b ^ 1
        keep = jnp.where(seg[b] == seg[o], 1.0, 0.0).astype(F32)
        here = slice(b * block_rows, (b + 1) * block_rows)
        there = slice(o * block_rows, (o + 1) * block_rows)

        @pl.loop(0, block_rows // TILE)
        def _(r):
            at = pl.ds(pl.multiple_of(b * block_rows + r * TILE, TILE), TILE)
            for a in range(heads):
                c = slice(a * dim, (a + 1) * dim)
                query = q_s[at, c]
                acc[a, at, :] = tile(query, k_hi[here, c], v_raw[here, c]) + keep * tile(
                    query, k_hi[there, c], v_raw[there, c]
                )

        if b == 0:
            for s in reversed(range(2, steps)):
                forward(s, 0)

    def far(s, a, at):
        level = local_levels + s
        c = slice(a * dim, (a + 1) * dim)
        cv = slice(width + a * dim, width + (a + 1) * dim)
        decay = jnp.exp(jnp.full((1, 2 * dim), -level * shift[a], F32))
        keys, values = recv[s][:, c].astype(BF16), recv[s][:, cv].astype(BF16)
        return acc[a, at, :] + decay * tile(q_s[at, c], keys, values)

    if steps > 1:
        forward(1, 0)
    for stage in range(1, steps):
        for s in reversed(range(stage + 1, steps)):
            forward(s, stage)
    last = min(1, steps - 1)
    for s in [s for s in [0, *reversed(range(2, steps))] if s != last]:
        kv_copies[s, s].wait_recv()

        @pl.loop(0, rows // TILE)
        def _(r):
            at = pl.ds(pl.multiple_of(r * TILE, TILE), TILE)
            for a in range(heads):
                acc[a, at, :] = far(s, a, at)

    kv_copies[last, last].wait_recv()

    def project(at, i):
        return dot(att[0, at, :], w_v[i, :width, :]) + dot(att[1, at, :], w_v[i, width:, :])

    att_copies, y_copies = [], []
    for r in range(len(chunks) + 1):
        if r < len(chunks):
            first, size = chunks[r]
            at = slice(first, first + size)
            for a in range(heads):
                total = far(last, a, at)
                att[0, at, a * dim : (a + 1) * dim] = (total[:, :dim] / total[:, dim:]).astype(BF16)
            copy = pltpu.make_async_remote_copy(
                src_ref=att.at[0, pl.ds(first, size)],
                dst_ref=att.at[1, pl.ds(first, size)],
                send_sem=att_send_sem.at[r],
                recv_sem=att_recv_sem.at[r],
                device_id={"head": h1},
                device_id_type=MESH,
            )
            copy.start()
            att_copies.append(copy)
        if r >= 1:
            if r == 1:
                for i in (1, 0):
                    w_loads[i].wait()
                    w_copies[i].wait_recv()
            att_copies[r - 1].wait_recv()
            first, size = chunks[r - 1]
            at = slice(first, first + size)
            y_send[at, :] = project(at, 1).astype(BF16)
            copy = pltpu.make_async_remote_copy(
                src_ref=y_send.at[pl.ds(first, size)],
                dst_ref=y_recv.at[pl.ds(first, size)],
                send_sem=y_send_sem.at[r - 1],
                recv_sem=y_recv_sem.at[r - 1],
                device_id={"head": h2},
                device_id_type=MESH,
            )
            copy.start()
            y_copies.append(copy)

    for first in range(0, rows, TILE):
        at = slice(first, first + TILE)
        own[at, :] = project(at, 0)
    for (first, size), copy in zip(chunks, y_copies):
        at = slice(first, first + size)
        copy.wait_recv()
        out_ref[at, :] = (own[at, :] + y_recv[at, :].astype(F32)).astype(BF16)

    for copy in list(kv_copies.values()) + w_copies + att_copies + y_copies:
        copy.wait_send()


def per_device(n_ctx, n_head, q, k, v, seg, factor, shift, weights):
    rows, width = q.shape
    heads = factor.shape[0]
    blocks = seg.shape[0]
    block_rows = rows // blocks
    out_cols = weights.shape[1] // n_head
    steps = n_ctx.bit_length() - 1
    chunks = len(row_chunks(rows))
    dim = width // heads
    hops = steps * (steps + 1) // 2

    def kind(s):
        return BF16 if (block_rows >> s) % 16 == 0 else F32

    hbm = pl.BlockSpec(memory_space=pltpu.HBM)
    smem = pl.BlockSpec(memory_space=pltpu.SMEM)
    dma = pltpu.SemaphoreType.DMA
    return pl.pallas_call(
        functools.partial(kernel, n_ctx, n_head, heads, blocks),
        out_shape=jax.ShapeDtypeStruct((rows, out_cols), BF16),
        in_specs=[hbm, hbm, hbm, smem, smem, smem, hbm],
        out_specs=pl.BlockSpec(memory_space=pltpu.VMEM),
        scratch_shapes=[
            *[pltpu.VMEM((rows, width), BF16)] * 5,
            pltpu.VMEM((rows, rows), BF16),
            pltpu.VMEM((heads, rows, 2 * dim), F32),
            pltpu.VMEM((2, rows, width), BF16),
            pltpu.VMEM((2, 2 * width, out_cols), BF16),
            pltpu.VMEM((rows, out_cols), BF16),
            pltpu.VMEM((rows, out_cols), BF16),
            pltpu.VMEM((rows, out_cols), F32),
            dma((5,)),
            dma((hops,)),
            dma((hops,)),
            dma((2,)),
            dma((2,)),
            dma((chunks,)),
            dma((chunks,)),
            dma((chunks,)),
            dma((chunks,)),
            *[pltpu.VMEM((block_rows >> s, 2 * width), kind(s)) for s in range(steps)],
            *[pltpu.VMEM((block_rows, 2 * width), kind(s)) for s in range(steps)],
        ],
        compiler_params=pltpu.CompilerParams(
            collective_id=0, has_side_effects=True, vmem_limit_bytes=64 * 1024 * 1024 - 65536
        ),
        cost_estimate=pl.CostEstimate(
            flops=4 * 10**9, bytes_accessed=8 * 10**6, transcendentals=3 * 10**6
        ),
    )(q, k, v, seg, factor, shift, weights)


def solution(mesh):
    placed = (
        P("ctx", "head"),
        P("ctx", "head"),
        P("ctx", "head"),
        P("ctx"),
        P("head"),
        P("head"),
        P("head", None),
    )
    body = functools.partial(per_device, mesh.shape["ctx"], mesh.shape["head"])
    return jax.shard_map(
        body, mesh=mesh, in_specs=placed, out_specs=P("ctx", "head"), check_vma=False
    )
```
